32 devices in a mesh: dp: 8 (over z, core), expert: 4 (over y, x).
Axes of the slice: x: 2, y: 2, z: 4, core: 2. Of those that a mesh axis runs over, the one named last changes fastest.
Arguments:
- tokens: bfloat16 [2048, 2048], P(('dp', 'expert')), parts along dimension 0, may hold values from -6 to 6
- router_weight: bfloat16 [2048, 4], replicated, may hold values from -0.125 to 0.125
- gate_weight: bfloat16 [4, 2048, 768], P('expert'), may hold values from -0.125 to 0.125
- up_weight: bfloat16 [4, 2048, 768], P('expert'), may hold values from -0.125 to 0.125
- down_weight: bfloat16 [4, 768, 2048], P('expert'), may hold values from -0.21875 to 0.21875
- routing: int32 [2048, 4], P(('dp', 'expert')), parts along dimension 0, may hold values from 0 to 3, as said below
- priority: int32 [32, 256], P(('dp', 'expert')), parts along dimension 0, may hold values from 0 to 255, each once within a row
- hot_list: int32 [16], P('dp'), parts along dimension 0, may hold values from 0 to 3, as said below
Outputs:
- mixed: bfloat16 [2048, 2048], P(('dp', 'expert')), parts along dimension 0
The draws below stay inside these ranges and needn't reach their ends.
There are 8 independent parts, one for each index of `dp`. The reference program is written for one: setup_inputs(seed, part) draws one part's arguments, and reference() takes and returns one part's arrays. A program takes and returns all parts, laid end to end along the dimension named above; an argument that names none is the same for every part. Nothing has to cross between parts.
Inputs may be any that keep to these rules, and one draw needn't show every extreme that they name: `routing`: each token names 4 different experts. `priority`: each row is a permutation. `hot_list`: 2 different experts.
All inputs are finite; a program needn't handle non-finite values.
Results may differ from the reference program's by a relative error of at most 0.0085.
Values may be sent and summed in bfloat16 or wider, within the bound.
No kernel may reach another device: no remote copies, remote signals or barrier semaphores. Data moves between devices by JAX's collectives and lax.ppermute only.
A program may use at most 64 MiB of HBM per device.

```python
import jax
import jax.numpy as jnp
from jax import lax

D = 2048
FF = 768
TOK_DEV = 64
TOPK = 4
HOT = 2
EXPERTS = 4
TOKENS = 256
SLOTS = 256
CAP = 64
N_EXPERT = 4


def routing_and_hot(key):
    base = jax.random.fold_in(key, 11)
    order = jax.random.permutation(jax.random.fold_in(base, 1), EXPERTS).astype(jnp.int32)
    place = jnp.argsort(order).astype(jnp.int32)
    pull = jnp.where(place < HOT, 3000, jnp.where(place < 2 * HOT, 2400, 1200 * (EXPERTS - place) // EXPERTS)).astype(jnp.int32)
    tickets = jax.random.randint(jax.random.fold_in(base, 2), (TOKENS, EXPERTS), 0, 4096, dtype=jnp.int32)
    labels = jnp.arange(EXPERTS, dtype=jnp.int32)
    scores = (tickets + pull[None, :]) * EXPERTS + labels[None, :]
    values, chosen = lax.top_k(scores, TOPK)
    return (chosen.astype(jnp.int32), order[:HOT])


def draw_routing(key, part):
    return routing_and_hot(key)[0]


def draw_hot_list(key, part):
    return routing_and_hot(key)[1]


def levels(stream_key, shape, pieces, smallest, high):
    gain = 1.0
    for axis_at, blocks in pieces:
        heights = jax.random.uniform(jax.random.fold_in(jax.random.fold_in(stream_key, 6), axis_at), (blocks,), jnp.float32, smallest / len(pieces), high / len(pieces))
        gain = gain * jnp.repeat(jnp.exp(heights), shape[axis_at] // blocks).reshape((-1,) + (1,) * (len(shape) - 1 - axis_at))
    return gain


def centred(stream_key, extent, spread, limit, shards=(), held_as=jnp.bfloat16):
    entries = jax.random.normal(stream_key, extent, jnp.float32) * spread
    if len(shards) > 0:
        entries = levels(stream_key, extent, shards, -0.22, 0.18) * entries
    return jnp.clip(entries, min=-limit, max=limit).astype(held_as)


def setup_inputs(seed: int = 0, part: int = 0) -> dict:
    splits = jax.random.split(jax.random.key(seed), 9)
    own_keys = jax.random.split(jax.random.fold_in(splits[8], part), 9)
    tokens = centred(own_keys[0], (TOKENS, D), 1.0, 6.0, ((0, 4),))
    router_weight = centred(splits[1], (D, EXPERTS), D ** -0.5, 0.125)
    gate_weight = centred(splits[2], (EXPERTS, D, FF), D ** -0.5, 0.125, ((0, 4),))
    up_weight = centred(splits[3], (EXPERTS, D, FF), D ** -0.5, 0.125, ((0, 4),))
    down_weight = centred(splits[4], (EXPERTS, FF, D), FF ** -0.5, 0.21875, ((0, 4),))
    routing = draw_routing(jax.random.fold_in(jax.random.fold_in(splits[8], part), 71), part)
    priority = jax.vmap(lambda own: jax.random.permutation(own, SLOTS))(jax.random.split(own_keys[6], N_EXPERT)).reshape((N_EXPERT, SLOTS)).astype(jnp.int32)
    hot_list = draw_hot_list(jax.random.fold_in(jax.random.fold_in(splits[8], part), 71), part)
    return dict(tokens=tokens, router_weight=router_weight, gate_weight=gate_weight, up_weight=up_weight, down_weight=down_weight, routing=routing, priority=priority, hot_list=hot_list)


def expert_swiglu(inputs, gate_mat, up_mat, down_mat):
    gate_part = jnp.dot(inputs, gate_mat, preferred_element_type=jnp.float32)
    up_part = jnp.dot(inputs, up_mat, preferred_element_type=jnp.float32)
    hidden = (jax.nn.silu(gate_part) * up_part).astype(jnp.bfloat16)
    return jnp.dot(hidden, down_mat, preferred_element_type=jnp.float32).astype(jnp.bfloat16)


def reference(tokens, router_weight, gate_weight, up_weight, down_weight, routing, priority, hot_list):
    logits = jnp.dot(tokens, router_weight, preferred_element_type=jnp.float32)
    chosen = jnp.take_along_axis(logits, routing, axis=1)
    sigmas = jax.nn.sigmoid(chosen)
    weights = sigmas / jnp.sum(sigmas, axis=1, keepdims=True)
    hot_flag = jnp.any(routing[:, :, None] == hot_list[None, None, :], axis=2)
    block_expert = routing.reshape(N_EXPERT, TOK_DEV * TOPK)
    block_hot = hot_flag.reshape(N_EXPERT, TOK_DEV * TOPK)
    same_expert = block_expert[:, :, None] == block_expert[:, None, :]
    earlier = priority[:, None, :] < priority[:, :, None]
    ranks = jnp.sum((same_expert & earlier).astype(jnp.int32), axis=2)
    keeping = block_hot | (ranks < CAP)
    kept = jnp.where(keeping.reshape(TOKENS, TOPK), weights, jnp.float32(0.0))

    def add_expert(index, total):
        answer = expert_swiglu(tokens, gate_weight[index], up_weight[index], down_weight[index])
        share = jnp.sum(jnp.where(routing == index, kept, jnp.float32(0.0)), axis=1)
        return total + share[:, None] * answer.astype(jnp.float32)

    total = lax.fori_loop(0, EXPERTS, add_expert, jnp.zeros((TOKENS, D), jnp.float32))
    return total.astype(jnp.bfloat16)
```

```python
import functools

import jax
import jax.numpy as jnp
from jax import lax
from jax.experimental import pallas as pl
from jax.experimental.pallas import tpu as pltpu
from jax.sharding import PartitionSpec as P

VMEM = pl.BlockSpec(memory_space=pltpu.VMEM)
SMEM = pl.BlockSpec(memory_space=pltpu.SMEM)
ROOM = 32 << 20


def share_kernel(capacity, peers, me_ref, hot_ref, tokens_ref, router_ref, routing_ref, priority_ref, share_ref):
    logits = jnp.dot(tokens_ref[...], router_ref[...], preferred_element_type=jnp.float32)
    sigmas = 1.0 / (1.0 + jnp.exp(-logits))
    routing = routing_ref[...]
    rows, top = routing.shape
    slots = rows * top
    experts = logits.shape[1]
    expert_at = lax.broadcasted_iota(jnp.int32, (rows, experts), 1)
    choice = lax.broadcasted_iota(jnp.int32, (rows, slots), 1) - top * lax.broadcasted_iota(
        jnp.int32, (rows, slots), 0
    )
    priority = jnp.broadcast_to(priority_ref[...], (rows, slots))
    columns = [routing[:, k : k + 1] for k in range(top)]
    slot_priority = [
        jnp.sum(jnp.where(choice == k, priority, 0), axis=1, keepdims=True) for k in range(top)
    ]
    slot_expert = jnp.zeros((1, slots), jnp.int32)
    total = jnp.zeros((rows, 1), jnp.float32)
    for k in range(top):
        slot_expert += jnp.sum(jnp.where(choice == k, columns[k], 0), axis=0, keepdims=True)
        total += jnp.sum(jnp.where(expert_at == columns[k], sigmas, 0.0), axis=1, keepdims=True)
    lane = lax.broadcasted_iota(jnp.int32, share_ref.shape, 1)
    share = jnp.zeros(share_ref.shape, jnp.float32)
    for d, peer in enumerate(peers):
        expert = peer(me_ref[0])
        here = jnp.zeros((rows, 1), jnp.int32)
        mine = jnp.zeros((rows, 1), jnp.int32)
        for k in range(top):
            at = columns[k] == expert
            here += at.astype(jnp.int32)
            mine += jnp.where(at, slot_priority[k], 0)
        rank = jnp.sum(
            ((slot_expert == expert) & (priority < mine)).astype(jnp.int32), axis=1, keepdims=True
        )
        hot = jnp.int32(0)
        for h in range(hot_ref.shape[0]):
            hot += (hot_ref[h] == expert).astype(jnp.int32)
        keeping = (here > 0) & ((rank < capacity) | (hot > 0))
        sigma = jnp.sum(jnp.where(expert_at == expert, sigmas, 0.0), axis=1, keepdims=True)
        share = jnp.where(lane == d, jnp.where(keeping, sigma / total, 0.0), share)
    share_ref[...] = share


def expert_kernel(inputs_ref, gate_ref, up_ref, down_ref, answer_ref):
    gate_part = jnp.dot(inputs_ref[...], gate_ref[0], preferred_element_type=jnp.float32)
    up_part = jnp.dot(inputs_ref[...], up_ref[0], preferred_element_type=jnp.float32)
    hidden = (gate_part / (1.0 + jnp.exp(-gate_part)) * up_part).astype(jnp.bfloat16)
    answer_ref[...] = jnp.dot(hidden, down_ref[0], preferred_element_type=jnp.float32).astype(
        answer_ref.dtype
    )


def mix_kernel(share_ref, *refs):
    *answers, mixed_ref = refs
    total = share_ref[:, 0:1] * answers[0][...].astype(jnp.float32)
    for d in range(1, len(answers)):
        total += share_ref[:, d : d + 1] * answers[d][...].astype(jnp.float32)
    mixed_ref[...] = total.astype(mixed_ref.dtype)


def call(kernel, shape, dtype, operands, specs=None, cost=None):
    return pl.pallas_call(
        kernel,
        out_shape=jax.ShapeDtypeStruct(shape, dtype),
        in_specs=specs or [VMEM] * len(operands),
        out_specs=VMEM,
        compiler_params=pltpu.CompilerParams(vmem_limit_bytes=ROOM),
        cost_estimate=cost,
    )(*operands)


def shards(tokens, router_weight, gate_weight, up_weight, down_weight, routing, priority, hot_list):
    devices_n = lax.axis_size("expert")
    tok_count, width = tokens.shape
    hidden_n = gate_weight.shape[2]
    slot_count = tok_count * routing.shape[1]
    capacity = min(tok_count, 3 * slot_count // (2 * devices_n))
    me = lax.axis_index("expert").astype(jnp.int32).reshape(1)
    if devices_n & (devices_n - 1) == 0:
        paths = [(lambda i, d=d: i ^ d) for d in range(devices_n)]
        backs = paths
    else:
        paths = [(lambda i, d=d: (i + d) % devices_n) for d in range(devices_n)]
        backs = [(lambda i, d=d: (i + devices_n - d) % devices_n) for d in range(devices_n)]

    def send(array, path):
        return lax.ppermute(array, "expert", [(i, path(i)) for i in range(devices_n)])

    def answer(rows):
        cost = pl.CostEstimate(
            flops=6 * rows.shape[0] * width * hidden_n, bytes_accessed=6 * width * hidden_n, transcendentals=0
        )
        return call(expert_kernel, rows.shape, rows.dtype, (rows, gate_weight, up_weight, down_weight), cost=cost)

    arrived = [send(tokens, paths[d]) for d in range(1, devices_n)]
    share = call(
        functools.partial(share_kernel, capacity, paths),
        (tok_count, 128),
        jnp.float32,
        (me, hot_list, tokens, router_weight, routing, priority),
        [SMEM, SMEM] + [VMEM] * 4,
    )
    answers = [answer(tokens)]
    for d in range(1, devices_n):
        answers.append(send(answer(arrived[d - 1]), backs[d]))
    return call(mix_kernel, tokens.shape, tokens.dtype, (share, *answers))


def solution(mesh):
    return jax.shard_map(
        shards,
        mesh=mesh,
        in_specs=(
            P(("dp", "expert"), None),
            P(),
            P("expert", None, None),
            P("expert", None, None),
            P("expert", None, None),
            P(("dp", "expert"), None),
            P(("dp", "expert"), None),
            P("dp"),
        ),
        out_specs=P(("dp", "expert"), None),
        check_vma=False,
    )
```

```python
import functools

import jax
import jax.numpy as jnp
from jax import lax
from jax.experimental import pallas as pl
from jax.experimental.pallas import tpu as pltpu
from jax.sharding import PartitionSpec as P

VMEM = pl.BlockSpec(memory_space=pltpu.VMEM)
SMEM = pl.BlockSpec(memory_space=pltpu.SMEM)
HBM = pl.BlockSpec(memory_space=pltpu.HBM)
ROOM = 24 << 20
FIRST_ROOM = 43 << 20
ANY = pl.BlockSpec(memory_space=pl.ANY)
LANES = 128


def kept_shares(capacity, peers, me, hot, tokens, router, routing, priority):
    logits = lax.dot_general(tokens, router, (((1,), (1,)), ((), ())), preferred_element_type=jnp.float32)
    sigmas = 1.0 / (1.0 + jnp.exp(-logits))
    top, rows = routing.shape
    slots = rows * top
    expert_at = lax.broadcasted_iota(jnp.int32, sigmas.shape, 1)
    choice = lax.broadcasted_iota(jnp.int32, (rows, slots), 1) - top * lax.broadcasted_iota(
        jnp.int32, (rows, slots), 0
    )
    square = lax.broadcasted_iota(jnp.int32, (rows, rows), 0) == lax.broadcasted_iota(jnp.int32, (rows, rows), 1)
    priority = jnp.broadcast_to(priority, (rows, slots))
    columns = [
        jnp.sum(jnp.where(square, routing[k : k + 1, :], 0), axis=1, keepdims=True) for k in range(top)
    ]
    slot_priority = [
        jnp.sum(jnp.where(choice == k, priority, 0), axis=1, keepdims=True) for k in range(top)
    ]
    slot_expert = jnp.zeros((1, slots), jnp.int32)
    total = jnp.zeros((rows, 1), jnp.float32)
    for k in range(top):
        slot_expert += jnp.sum(jnp.where(choice == k, columns[k], 0), axis=0, keepdims=True)
        total += jnp.sum(jnp.where(expert_at == columns[k], sigmas, 0.0), axis=1, keepdims=True)
    lane = lax.broadcasted_iota(jnp.int32, (rows, LANES), 1)
    share = jnp.zeros((rows, LANES), jnp.float32)
    for d, peer in enumerate(peers):
        expert = peer(me)
        here = jnp.zeros((rows, 1), jnp.int32)
        mine = jnp.zeros((rows, 1), jnp.int32)
        for k in range(top):
            at = columns[k] == expert
            here += at.astype(jnp.int32)
            mine += jnp.where(at, slot_priority[k], 0)
        rank = jnp.sum(
            ((slot_expert == expert) & (priority < mine)).astype(jnp.int32), axis=1, keepdims=True
        )
        is_hot = jnp.int32(0)
        for h in hot:
            is_hot += (h == expert).astype(jnp.int32)
        keeping = (here > 0) & ((rank < capacity) | (is_hot > 0))
        sigma = jnp.sum(jnp.where(expert_at == expert, sigmas, 0.0), axis=1, keepdims=True)
        share = jnp.where(lane == d, jnp.where(keeping, sigma / total, 0.0), share)
    return share


def swiglu(inputs, gate, up, down):
    gate_part = jnp.dot(inputs, gate(), preferred_element_type=jnp.float32)
    up_part = jnp.dot(inputs, up(), preferred_element_type=jnp.float32)
    hidden = (gate_part / (1.0 + jnp.exp(-gate_part)) * up_part).astype(jnp.bfloat16)
    return jnp.dot(hidden, down(), preferred_element_type=jnp.float32)


def share_kernel(capacity, peers, me_ref, hot_ref, tokens_ref, router_ref, routing_ref, priority_ref, *refs):
    hot = [hot_ref[h] for h in range(hot_ref.shape[0])]
    refs[-1][...] = kept_shares(
        capacity, peers, me_ref[0], hot, tokens_ref[...], router_ref[...], routing_ref[...], priority_ref[...]
    )


def first_kernel(tokens_ref, gate_in, up_in, down_in, own_ref, gate_ref, up_ref, down_ref, sems):
    pairs = [(gate_in, gate_ref), (up_in, up_ref), (down_in, down_ref)]
    copies = [pltpu.make_async_copy(src, dst, sems.at[i]) for i, (src, dst) in enumerate(pairs)]
    for copy in copies:
        copy.start()

    def landed(copy, ref):
        def get():
            copy.wait()
            return ref[0]

        return get

    weights = [landed(copy, ref) for copy, (_, ref) in zip(copies, pairs)]
    own_ref[...] = swiglu(tokens_ref[...], *weights).astype(own_ref.dtype)


def expert_kernel(count, *refs):
    inputs, (gate_ref, up_ref, down_ref), answers = refs[:count], refs[count : count + 3], refs[-count:]
    rows = [ref[...] for ref in inputs]
    result = swiglu(
        rows[0] if count == 1 else jnp.concatenate(rows), lambda: gate_ref[0], lambda: up_ref[0], lambda: down_ref[0]
    ).astype(answers[0].dtype)
    step = rows[0].shape[0]
    for i, ref in enumerate(answers):
        ref[...] = result[i * step : (i + 1) * step]


def mix_kernel(share_ref, *refs):
    *answers, mixed_ref = refs
    total = share_ref[:, 0:1] * answers[0][...].astype(jnp.float32)
    for d in range(1, len(answers)):
        total += share_ref[:, d : d + 1] * answers[d][...].astype(jnp.float32)
    mixed_ref[...] = total.astype(mixed_ref.dtype)


def call(kernel, outs, operands, specs=None, scratch=(), cost=None, room=ROOM):
    return pl.pallas_call(
        kernel,
        out_shape=outs,
        in_specs=specs or [VMEM] * len(operands),
        out_specs=jax.tree.map(lambda _: VMEM, outs),
        scratch_shapes=scratch,
        compiler_params=pltpu.CompilerParams(vmem_limit_bytes=room),
        cost_estimate=cost,
    )(*operands)


def groups(devices_n):
    order = list(range(devices_n - 1, 0, -1))
    return [order[:1]] + [order[i : i + 2] for i in range(1, len(order), 2)]


def shards(tokens, router_weight, gate_weight, up_weight, down_weight, routing, priority, hot_list):
    devices_n = lax.axis_size("expert")
    tok_count, width = tokens.shape
    top_count = routing.shape[1]
    hidden_n = gate_weight.shape[2]
    slot_count = tok_count * top_count
    capacity = min(tok_count, 3 * slot_count // (2 * devices_n))
    me = lax.axis_index("expert").astype(jnp.int32).reshape(1)
    if devices_n & (devices_n - 1) == 0:
        paths = [(lambda i, d=d: i ^ d) for d in range(devices_n)]
        backs = paths
    else:
        paths = [(lambda i, d=d: (i + d) % devices_n) for d in range(devices_n)]
        backs = [(lambda i, d=d: (i + devices_n - d) % devices_n) for d in range(devices_n)]

    def send(array, path):
        return lax.ppermute(array, "expert", [(i, path(i)) for i in range(devices_n)])

    def like(array):
        return jax.ShapeDtypeStruct(array.shape, array.dtype)

    def cost(rows):
        return pl.CostEstimate(
            flops=6 * rows * width * hidden_n, bytes_accessed=6 * width * hidden_n, transcendentals=0
        )

    def experts(blocks, weights, after=()):
        count = len(blocks)
        return call(
            functools.partial(expert_kernel, count),
            (like(tokens),) * count,
            (*blocks, *weights, *after),
            [VMEM] * (count + 3) + [ANY] * len(after),
            cost=cost(tok_count * count),
        )

    order = range(devices_n - 1, 0, -1)
    arrived = {d: send(tokens, paths[d]) for d in order}
    own, *weights = call(
        first_kernel,
        (like(tokens), like(gate_weight), like(up_weight), like(down_weight)),
        (tokens, gate_weight, up_weight, down_weight),
        [VMEM, HBM, HBM, HBM],
        [pltpu.SemaphoreType.DMA((3,))],
        cost(tok_count),
        FIRST_ROOM,
    )
    answers = {0: own}
    last = ()
    for group in groups(devices_n):
        results = experts([arrived[d] for d in group], weights)
        last = results[:1]
        for d, result in zip(group, results):
            answers[d] = send(result, backs[d])
    share = call(
        functools.partial(share_kernel, capacity, paths),
        jax.ShapeDtypeStruct((tok_count, LANES), jnp.float32),
        (me, hot_list, tokens, router_weight.T, routing.T, priority, *last),
        [SMEM, SMEM] + [VMEM] * 4 + [ANY] * len(last),
    )
    return call(mix_kernel, like(tokens), (share, *[answers[d] for d in range(devices_n)]))


def solution(mesh):
    return jax.shard_map(
        shards,
        mesh=mesh,
        in_specs=(
            P(("dp", "expert"), None),
            P(),
            P("expert", None, None),
            P("expert", None, None),
            P("expert", None, None),
            P(("dp", "expert"), None),
            P(("dp", "expert"), None),
            P("dp"),
        ),
        out_specs=P(("dp", "expert"), None),
        check_vma=False,
    )
```

```python
import functools

import jax
import jax.numpy as jnp
from jax import lax
from jax.experimental import pallas as pl
from jax.experimental.pallas import tpu as pltpu
from jax.sharding import PartitionSpec as P

VMEM = pl.BlockSpec(memory_space=pltpu.VMEM)
SMEM = pl.BlockSpec(memory_space=pltpu.SMEM)
HBM = pl.BlockSpec(memory_space=pltpu.HBM)
ROOM = 24 << 20
FIRST_ROOM = 43 << 20
ANY = pl.BlockSpec(memory_space=pl.ANY)
LANES = 128


def kept_shares(capacity, peers, me, hot, tokens, router, routing, priority):
    logits = lax.dot_general(tokens, router, (((1,), (1,)), ((), ())), preferred_element_type=jnp.float32)
    sigmas = 1.0 / (1.0 + jnp.exp(-logits))
    top, rows = routing.shape
    slots = rows * top
    expert_at = lax.broadcasted_iota(jnp.int32, sigmas.shape, 1)
    choice = lax.broadcasted_iota(jnp.int32, (rows, slots), 1) - top * lax.broadcasted_iota(
        jnp.int32, (rows, slots), 0
    )
    square = lax.broadcasted_iota(jnp.int32, (rows, rows), 0) == lax.broadcasted_iota(jnp.int32, (rows, rows), 1)
    priority = jnp.broadcast_to(priority, (rows, slots))
    columns = [
        jnp.sum(jnp.where(square, routing[k : k + 1, :], 0), axis=1, keepdims=True) for k in range(top)
    ]
    slot_priority = [
        jnp.sum(jnp.where(choice == k, priority, 0), axis=1, keepdims=True) for k in range(top)
    ]
    slot_expert = jnp.zeros((1, slots), jnp.int32)
    total = jnp.zeros((rows, 1), jnp.float32)
    for k in range(top):
        slot_expert += jnp.sum(jnp.where(choice == k, columns[k], 0), axis=0, keepdims=True)
        total += jnp.sum(jnp.where(expert_at == columns[k], sigmas, 0.0), axis=1, keepdims=True)
    lane = lax.broadcasted_iota(jnp.int32, (rows, LANES), 1)
    share = jnp.zeros((rows, LANES), jnp.float32)
    for d, peer in enumerate(peers):
        expert = peer(me)
        here = jnp.zeros((rows, 1), jnp.int32)
        mine = jnp.zeros((rows, 1), jnp.int32)
        for k in range(top):
            at = columns[k] == expert
            here += at.astype(jnp.int32)
            mine += jnp.where(at, slot_priority[k], 0)
        rank = jnp.sum(
            ((slot_expert == expert) & (priority < mine)).astype(jnp.int32), axis=1, keepdims=True
        )
        is_hot = jnp.int32(0)
        for h in hot:
            is_hot += (h == expert).astype(jnp.int32)
        keeping = (here > 0) & ((rank < capacity) | (is_hot > 0))
        sigma = jnp.sum(jnp.where(expert_at == expert, sigmas, 0.0), axis=1, keepdims=True)
        share = jnp.where(lane == d, jnp.where(keeping, sigma / total, 0.0), share)
    return share


def swiglu(inputs, gate, up, down):
    gate_part = jnp.dot(inputs, gate(), preferred_element_type=jnp.float32)
    up_part = jnp.dot(inputs, up(), preferred_element_type=jnp.float32)
    hidden = (gate_part / (1.0 + jnp.exp(-gate_part)) * up_part).astype(jnp.bfloat16)
    return jnp.dot(hidden, down(), preferred_element_type=jnp.float32)


def share_kernel(capacity, peers, me_ref, hot_ref, tokens_ref, router_ref, routing_ref, priority_ref, *refs):
    hot = [hot_ref[h] for h in range(hot_ref.shape[0])]
    refs[-1][...] = kept_shares(
        capacity, peers, me_ref[0], hot, tokens_ref[...], router_ref[...], routing_ref[...], priority_ref[...]
    )


def load_kernel(*refs):
    count = (len(refs) - 1) // 2
    sources, targets, sems = refs[:count], refs[count : 2 * count], refs[-1]
    copies = [pltpu.make_async_copy(src, dst, sems.at[i]) for i, (src, dst) in enumerate(zip(sources, targets))]
    for copy in copies:
        copy.start()
    for copy in copies:
        copy.wait()


def expert_kernel(count, *refs):
    inputs, (gate_ref, up_ref, down_ref), answers = refs[:count], refs[count : count + 3], refs[-count:]
    rows = [ref[...] for ref in inputs]
    result = swiglu(
        rows[0] if count == 1 else jnp.concatenate(rows), lambda: gate_ref[0], lambda: up_ref[0], lambda: down_ref[0]
    ).astype(answers[0].dtype)
    step = rows[0].shape[0]
    for i, ref in enumerate(answers):
        ref[...] = result[i * step : (i + 1) * step]


def weigh(share_ref, column, refs, total):
    for d, ref in enumerate(refs):
        term = share_ref[:, column + d : column + d + 1] * ref[...].astype(jnp.float32)
        total = term if total is None else total + term
    return total


def gather_kernel(columns, share_ref, *refs):
    total = None
    for column, ref in zip(columns, refs):
        total = weigh(share_ref, column, [ref], total)
    refs[-1][...] = total


def mix_kernel(columns, share_ref, total_ref, *refs):
    total = total_ref[...]
    for column, ref in zip(columns, refs):
        total = weigh(share_ref, column, [ref], total)
    refs[-1][...] = total.astype(refs[-1].dtype)


def call(kernel, outs, operands, specs=None, scratch=(), cost=None, room=ROOM):
    return pl.pallas_call(
        kernel,
        out_shape=outs,
        in_specs=specs or [VMEM] * len(operands),
        out_specs=jax.tree.map(lambda _: VMEM, outs),
        scratch_shapes=scratch,
        compiler_params=pltpu.CompilerParams(vmem_limit_bytes=room),
        cost_estimate=cost,
    )(*operands)


def groups(devices_n):
    order = list(range(devices_n - 1, 0, -1))
    return [order[:1]] + [order[i : i + 2][::-1] for i in range(1, len(order), 2)]


def shards(tokens, router_weight, gate_weight, up_weight, down_weight, routing, priority, hot_list):
    devices_n = lax.axis_size("expert")
    tok_count, width = tokens.shape
    top_count = routing.shape[1]
    hidden_n = gate_weight.shape[2]
    slot_count = tok_count * top_count
    capacity = min(tok_count, 3 * slot_count // (2 * devices_n))
    me = lax.axis_index("expert").astype(jnp.int32).reshape(1)
    if devices_n & (devices_n - 1) == 0:
        paths = [(lambda i, d=d: i ^ d) for d in range(devices_n)]
        backs = paths
    else:
        paths = [(lambda i, d=d: (i + d) % devices_n) for d in range(devices_n)]
        backs = [(lambda i, d=d: (i + devices_n - d) % devices_n) for d in range(devices_n)]

    def send(array, path):
        return lax.ppermute(array, "expert", [(i, path(i)) for i in range(devices_n)])

    def like(array):
        return jax.ShapeDtypeStruct(array.shape, array.dtype)

    def cost(rows):
        return pl.CostEstimate(
            flops=6 * rows * width * hidden_n, bytes_accessed=6 * width * hidden_n, transcendentals=0
        )

    def experts(blocks, weights, after=()):
        count = len(blocks)
        return call(
            functools.partial(expert_kernel, count),
            (like(tokens),) * count,
            (*blocks, *weights, *after),
            [VMEM] * (count + 3) + [ANY] * len(after),
            cost=cost(tok_count * count),
        )

    order = range(devices_n - 1, 0, -1)
    arrived = {d: send(tokens, paths[d]) for d in order}
    def load(arrays):
        size = sum(a.size for a in arrays) * 4
        return call(
            load_kernel,
            [like(a) for a in arrays],
            arrays,
            [HBM] * len(arrays),
            [pltpu.SemaphoreType.DMA((len(arrays),))],
            pl.CostEstimate(flops=0, bytes_accessed=size, transcendentals=0),
            FIRST_ROOM,
        )

    weights = load([gate_weight, up_weight, down_weight])
    arrived[0] = tokens
    answers = {}
    last = ()
    first, *others = groups(devices_n)
    for group in [*others, [0, *first]]:
        results = experts([arrived[d] for d in group], weights)
        last = results[:1]
        for d, result in zip(group, results):
            answers[d] = send(result, backs[d]) if d else result
    share = call(
        functools.partial(share_kernel, capacity, paths),
        jax.ShapeDtypeStruct((tok_count, LANES), jnp.float32),
        (me, hot_list, tokens, router_weight.T, routing.T, priority, *last),
        [SMEM, SMEM] + [VMEM] * 4 + [ANY] * len(last),
    )
    late, early = first, [0, *sum(others, [])]
    total = call(
        functools.partial(gather_kernel, early),
        jax.ShapeDtypeStruct(tokens.shape, jnp.float32),
        (share, *[answers[d] for d in early]),
    )
    return call(functools.partial(mix_kernel, late), like(tokens), (share, total, *[answers[d] for d in late]))


def solution(mesh):
    return jax.shard_map(
        shards,
        mesh=mesh,
        in_specs=(
            P(("dp", "expert"), None),
            P(),
            P("expert", None, None),
            P("expert", None, None),
            P("expert", None, None),
            P(("dp", "expert"), None),
            P(("dp", "expert"), None),
            P("dp"),
        ),
        out_specs=P(("dp", "expert"), None),
        check_vma=False,
    )
```

```python
import functools

import jax
import jax.numpy as jnp
from jax import lax
from jax.experimental import pallas as pl
from jax.experimental.pallas import tpu as pltpu
from jax.sharding import PartitionSpec as P

VMEM = pl.BlockSpec(memory_space=pltpu.VMEM)
SMEM = pl.BlockSpec(memory_space=pltpu.SMEM)
HBM = pl.BlockSpec(memory_space=pltpu.HBM)
ROOM = 24 << 20
FIRST_ROOM = 43 << 20
ANY = pl.BlockSpec(memory_space=pl.ANY)
LANES = 128


def kept_shares(capacity, peers, hot, tokens, router, routing, priority):
    logits = lax.dot_general(tokens, router, (((1,), (1,)), ((), ())), preferred_element_type=jnp.float32)
    sigmas = 1.0 / (1.0 + jnp.exp(-logits))
    top, rows = routing.shape
    slots = rows * top
    expert_at = lax.broadcasted_iota(jnp.int32, sigmas.shape, 1)
    choice = lax.broadcasted_iota(jnp.int32, (rows, slots), 1) - top * lax.broadcasted_iota(
        jnp.int32, (rows, slots), 0
    )
    square = lax.broadcasted_iota(jnp.int32, (rows, rows), 0) == lax.broadcasted_iota(jnp.int32, (rows, rows), 1)
    priority = jnp.broadcast_to(priority, (rows, slots))
    columns = [
        jnp.sum(jnp.where(square, routing[k : k + 1, :], 0), axis=1, keepdims=True) for k in range(top)
    ]
    slot_priority = [
        jnp.sum(jnp.where(choice == k, priority, 0), axis=1, keepdims=True) for k in range(top)
    ]
    slot_expert = jnp.zeros((1, slots), jnp.int32)
    total = jnp.zeros((rows, 1), jnp.float32)
    for k in range(top):
        slot_expert += jnp.sum(jnp.where(choice == k, columns[k], 0), axis=0, keepdims=True)
        total += jnp.sum(jnp.where(expert_at == columns[k], sigmas, 0.0), axis=1, keepdims=True)
    lane = lax.broadcasted_iota(jnp.int32, (rows, LANES), 1)
    share = jnp.zeros((rows, LANES), jnp.float32)
    for d, expert in enumerate(peers):
        here = jnp.zeros((rows, 1), jnp.int32)
        mine = jnp.zeros((rows, 1), jnp.int32)
        for k in range(top):
            at = columns[k] == expert
            here += at.astype(jnp.int32)
            mine += jnp.where(at, slot_priority[k], 0)
        rank = jnp.sum(
            ((slot_expert == expert) & (priority < mine)).astype(jnp.int32), axis=1, keepdims=True
        )
        is_hot = jnp.int32(0)
        for h in hot:
            is_hot += (h == expert).astype(jnp.int32)
        keeping = (here > 0) & ((rank < capacity) | (is_hot > 0))
        sigma = jnp.sum(jnp.where(expert_at == expert, sigmas, 0.0), axis=1, keepdims=True)
        share = jnp.where(lane == d, jnp.where(keeping, sigma / total, 0.0), share)
    return share


def swiglu(inputs, gate, up, down):
    gate_part = jnp.dot(inputs, gate(), preferred_element_type=jnp.float32)
    up_part = jnp.dot(inputs, up(), preferred_element_type=jnp.float32)
    hidden = (gate_part / (1.0 + jnp.exp(-gate_part)) * up_part).astype(jnp.bfloat16)
    return jnp.dot(hidden, down(), preferred_element_type=jnp.float32)


def share_kernel(capacity, peers_ref, hot_ref, tokens_ref, router_ref, routing_ref, priority_ref, *refs):
    peers = [peers_ref[d] for d in range(peers_ref.shape[0])]
    hot = [hot_ref[h] for h in range(hot_ref.shape[0])]
    refs[-1][...] = kept_shares(
        capacity, peers, hot, tokens_ref[...], router_ref[...], routing_ref[...], priority_ref[...]
    )


def first_kernel(gate_in, up_in, down_in, gate_ref, up_ref, down_ref, sems):
    pairs = [(gate_in, gate_ref), (up_in, up_ref), (down_in, down_ref)]
    copies = [pltpu.make_async_copy(src, dst, sems.at[i]) for i, (src, dst) in enumerate(pairs)]
    for copy in copies:
        copy.start()
    for copy in copies:
        copy.wait()


def expert_kernel(count, *refs):
    inputs, (gate_ref, up_ref, down_ref), answers = refs[:count], refs[count : count + 3], refs[-count:]
    rows = [ref[...] for ref in inputs]
    result = swiglu(
        rows[0] if count == 1 else jnp.concatenate(rows), lambda: gate_ref[0], lambda: up_ref[0], lambda: down_ref[0]
    ).astype(answers[0].dtype)
    step = rows[0].shape[0]
    for i, ref in enumerate(answers):
        ref[...] = result[i * step : (i + 1) * step]


def weigh(share_ref, column, refs, total):
    for d, ref in enumerate(refs):
        term = share_ref[:, column + d : column + d + 1] * ref[...].astype(jnp.float32)
        total = term if total is None else total + term
    return total


def gather_kernel(columns, share_ref, *refs):
    total = None
    for column, ref in zip(columns, refs):
        total = weigh(share_ref, column, [ref], total)
    refs[-1][...] = total


def mix_kernel(columns, share_ref, total_ref, *refs):
    total = total_ref[...]
    for column, ref in zip(columns, refs):
        total = weigh(share_ref, column, [ref], total)
    refs[-1][...] = total.astype(refs[-1].dtype)


def call(kernel, outs, operands, specs=None, scratch=(), cost=None, room=ROOM):
    return pl.pallas_call(
        kernel,
        out_shape=outs,
        in_specs=specs or [VMEM] * len(operands),
        out_specs=jax.tree.map(lambda _: VMEM, outs),
        scratch_shapes=scratch,
        compiler_params=pltpu.CompilerParams(vmem_limit_bytes=room),
        cost_estimate=cost,
    )(*operands)


def flipped(slot, devices_n):
    bits = devices_n.bit_length() - 1
    return sum(((slot >> b) & 1) << (bits - 1 - b) for b in range(bits))


def shards(tokens, router_weight, gate_weight, up_weight, down_weight, routing, priority, hot_list):
    devices_n, batches_n = lax.axis_size("expert"), lax.axis_size("dp")
    tok_count, width = tokens.shape
    top_count = routing.shape[1]
    hidden_n = gate_weight.shape[2]
    slot_count = tok_count * top_count
    capacity = min(tok_count, 3 * slot_count // (2 * devices_n))
    powers = devices_n & (devices_n - 1) == 0

    def there(slot, batch, expert):
        if powers:
            return expert ^ (flipped(slot, devices_n) if batch % 2 else slot)
        return (expert + slot) % devices_n

    def send(array, slot, back=False):
        pairs = [
            (b * devices_n + e, b * devices_n + there(slot, b, e)) for b in range(batches_n) for e in range(devices_n)
        ]
        return lax.ppermute(array, ("dp", "expert"), [(d, s) for s, d in pairs] if back else pairs)

    def like(array):
        return jax.ShapeDtypeStruct(array.shape, array.dtype)

    def cost(rows):
        return pl.CostEstimate(
            flops=6 * rows * width * hidden_n, bytes_accessed=6 * width * hidden_n, transcendentals=0
        )

    def experts(blocks, weights):
        count = len(blocks)
        return call(
            functools.partial(expert_kernel, count),
            (like(tokens),) * count,
            (*blocks, *weights),
            cost=cost(tok_count * count),
        )

    me = lax.axis_index("expert").astype(jnp.int32)
    odd = lax.axis_index("dp").astype(jnp.int32) % 2
    tables = [
        jnp.array([[there(slot, b, e) for slot in range(devices_n)] for e in range(devices_n)], jnp.int32) for b in (0, 1)
    ]
    peers = jnp.where(odd == 0, tables[0][me], tables[1][me])

    arrived = {0: tokens}
    weights = call(
        first_kernel,
        (like(gate_weight), like(up_weight), like(down_weight)),
        (gate_weight, up_weight, down_weight),
        [HBM] * 3,
        [pltpu.SemaphoreType.DMA((3,))],
        pl.CostEstimate(flops=0, bytes_accessed=12 * width * hidden_n, transcendentals=0),
        FIRST_ROOM,
    )
    near = [slot for slot in range(1, devices_n) if not powers or slot & (slot - 1) == 0]
    far = [slot for slot in range(1, devices_n) if slot not in near]
    for slot in near:
        arrived[slot] = send(tokens, slot)
    for slot in far:
        arrived[slot] = send(tokens, slot)
    answers = {}
    for slots in [near[i : i + 2][::-1] for i in range(0, len(near), 2)] + [([0] + far)[i : i + 2] for i in range(0, len(far) + 1, 2)]:
        for slot, result in zip(slots, experts([arrived[slot] for slot in slots], weights)):
            answers[slot] = send(result, slot, back=True) if slot else result
    share = call(
        functools.partial(share_kernel, capacity),
        jax.ShapeDtypeStruct((tok_count, LANES), jnp.float32),
        (peers, hot_list, tokens, router_weight.T, routing.T, priority, answers[0]),
        [SMEM, SMEM] + [VMEM] * 4 + [ANY],
    )
    early, late = list(range(devices_n - 1)), [devices_n - 1]
    total = call(
        functools.partial(gather_kernel, early),
        jax.ShapeDtypeStruct(tokens.shape, jnp.float32),
        (share, *[answers[d] for d in early]),
    )
    return call(functools.partial(mix_kernel, late), like(tokens), (share, total, *[answers[d] for d in late]))


def solution(mesh):
    return jax.shard_map(
        shards,
        mesh=mesh,
        in_specs=(
            P(("dp", "expert"), None),
            P(),
            P("expert", None, None),
            P("expert", None, None),
            P("expert", None, None),
            P(("dp", "expert"), None),
            P(("dp", "expert"), None),
            P("dp"),
        ),
        out_specs=P(("dp", "expert"), None),
        check_vma=False,
    )
```
